32 devices in a mesh: grp: 2 (over y), row: 4 (over x, core), col: 4 (over z).
Axes of the slice: x: 2, y: 2, z: 4, core: 2. Of those that a mesh axis runs over, the one named last changes fastest.
Arguments:
- amplitudes: bfloat16 [32768, 16384], P(('grp', 'row'), 'col'), parts along dimension 0, may hold values from -0.046875 to 0.046875
- cholesky: bfloat16 [1024, 32768], P('row', ('grp', 'col')), parts along dimension 1, may hold values from -1.078125 to 1.078125
- occ_index: int32 [32768], P('grp'), parts along dimension 0, may hold values from 0 to 31
- vir_index: int32 [32768], P('grp'), parts along dimension 0, may hold values from 0 to 511
- eps_occ: float32 [64], P('grp'), parts along dimension 0, may hold values from -2 to -0.3
- eps_vir: float32 [1024], P('grp'), parts along dimension 0, may hold values from 0.2 to 3
Outputs:
- new_amplitudes: bfloat16 [32768, 16384], P(('grp', 'row'), 'col'), parts along dimension 0
The draws below stay inside these ranges and needn't reach their ends.
There are 2 independent parts, one for each index of `grp`. The reference program is written for one: setup_inputs(seed, part) draws one part's arguments, and reference() takes and returns one part's arrays. A program takes and returns all parts, laid end to end along the dimension named above; each array names one. Nothing has to cross between parts.
All inputs are finite; a program needn't handle non-finite values.
Results may differ from the reference program's by a relative error of at most 0.0056.
Values may be sent and summed in bfloat16 or wider, within the bound.
No kernel may reach another device: no remote copies, remote signals or barrier semaphores. Data moves between devices by JAX's collectives and lax.ppermute only.
A program may use at most 128 MiB of HBM per device.

```python
import math
import jax
import jax.numpy as jnp
from jax import lax

NOCC = 32
NVIR = 512
NAUX = 1024
P_SIZE = 16384


def place_ends(drawn, own_key, least, largest):
    dims = drawn.shape
    index_at = [jax.random.randint(jax.random.fold_in(own_key, axis), (), 0, dims[axis]) for axis in range(len(dims))]
    drawn = drawn.at[tuple(index_at)].set(least)
    longest = dims.index(max(dims))
    index_at[longest] = (index_at[longest] + 1) % dims[longest]
    return drawn.at[tuple(index_at)].set(largest)


def steps_of(stream_key, shape, pieces, least, top_value):
    factor_of, own = 1.0, jax.random.fold_in(stream_key, 6)
    for axis_at, parts in pieces:
        heights = jnp.exp(jax.random.uniform(jax.random.fold_in(own, axis_at), (parts,), jnp.float32, least / len(pieces), top_value / len(pieces)))
        factor_of = factor_of * jnp.repeat(heights, shape[axis_at] // parts).reshape([-1 if axis == axis_at else 1 for axis in range(len(shape))])
    return factor_of


def gaussian(rng, extent, scale, limit, shards=(), kind=jnp.bfloat16):
    entries = scale * jax.random.normal(rng, extent, jnp.float32)
    if shards:
        entries = entries * steps_of(rng, extent, shards, -0.22, 0.18)
    return jnp.clip(entries, -limit, limit).astype(kind)


def setup_inputs(seed: int = 0, part: int = 0) -> dict:
    splits = jax.random.split(jax.random.key(seed), 7)
    part_splits = jax.random.split(jax.random.fold_in(splits[6], part), 7)
    return {
        "amplitudes": gaussian(part_splits[0], (P_SIZE, P_SIZE), P_SIZE ** -0.5, 0.046875, ((0, 4), (1, 4))),
        "cholesky": gaussian(part_splits[1], (NAUX, P_SIZE), 0.18, 1.078125, ((0, 4), (1, 4))),
        "occ_index": place_ends(jax.random.randint(part_splits[2], (P_SIZE,), 0, NOCC), jax.random.fold_in(part_splits[2], 1), 0, NOCC - 1).astype(jnp.int32),
        "vir_index": place_ends(jax.random.randint(part_splits[3], (P_SIZE,), 0, NVIR), jax.random.fold_in(part_splits[3], 1), 0, NVIR - 1).astype(jnp.int32),
        "eps_occ": jnp.clip(jax.random.uniform(part_splits[4], (NOCC,), jnp.float32, -2.0, -0.3), -2.0, -0.3),
        "eps_vir": jnp.clip(jax.random.uniform(part_splits[5], (NVIR,), jnp.float32, 0.2, 3.0), 0.2, 3.0),
    }


def reference(amplitudes, cholesky, occ_index, vir_index, eps_occ, eps_vir):
    gap = eps_vir[vir_index] - eps_occ[occ_index]
    dressed = jnp.dot(cholesky, amplitudes, preferred_element_type=jnp.float32)
    ydress = (cholesky.astype(jnp.float32) + dressed).astype(jnp.bfloat16)
    width = math.gcd(P_SIZE, 1024)

    def gram_block(block_id):
        columns = lax.dynamic_slice_in_dim(ydress, block_id * width, width, 1)
        gram = lax.dot_general(columns, ydress, (((0,), (0,)), ((), ())), preferred_element_type=jnp.float32)
        gaps = lax.dynamic_slice_in_dim(gap, block_id * width, width, 0)
        return (-gram / (gaps[:, None] + gap[None, :])).astype(jnp.bfloat16)

    blocks = lax.map(gram_block, jnp.arange(P_SIZE // width, dtype=jnp.int32))
    return blocks.reshape(P_SIZE, P_SIZE)
```

```python
import jax
import jax.numpy as jnp
from jax import lax
from jax.experimental import pallas as pl
from jax.experimental.pallas import tpu as pltpu
from jax.sharding import PartitionSpec as P

AXES = ("row", "col")
BF16 = jnp.bfloat16
F32 = jnp.float32


def pair_gaps(occ_index, vir_index, eps_occ, eps_vir, begin_pair, pair_count):
    occ_rows = lax.dynamic_slice_in_dim(occ_index, begin_pair, pair_count, 0)
    vir_rows = lax.dynamic_slice_in_dim(vir_index, begin_pair, pair_count, 0)
    occ_table = jnp.arange(eps_occ.shape[0], dtype=jnp.int32)
    vir_table = jnp.arange(eps_vir.shape[0], dtype=jnp.int32)
    occ_energy = jnp.sum(
        jnp.where(occ_rows[:, None] == occ_table[None, :], eps_occ[None, :], 0.0), axis=1
    )
    vir_energy = jnp.sum(
        jnp.where(vir_rows[:, None] == vir_table[None, :], eps_vir[None, :], 0.0), axis=1
    )
    return vir_energy - occ_energy


def general(amplitudes, cholesky, occ_index, vir_index, eps_occ, eps_vir):
    row_position = lax.axis_index("row")
    col_position = lax.axis_index("col")
    rows_block, cols_block = amplitudes.shape
    all_pairs = lax.all_gather(cholesky, "col", axis=1, tiled=True)
    chol_rows = lax.all_to_all(all_pairs, "row", split_axis=1, concat_axis=0, tiled=True)
    dressed = lax.psum_scatter(
        jnp.dot(chol_rows, amplitudes, preferred_element_type=F32),
        "row",
        scatter_dimension=0,
        tiled=True,
    )
    ydress = (cholesky.astype(F32) + dressed).astype(BF16)
    contract = (((0,), (0,)), ((), ()))
    ydress_pairs = lax.all_gather(ydress, "col", axis=1, tiled=True)
    ydress_rows = lax.all_to_all(ydress_pairs, "row", split_axis=1, concat_axis=0, tiled=True)
    gram = lax.dot_general(
        ydress_rows,
        lax.all_gather(ydress, "row", axis=0, tiled=True),
        contract,
        preferred_element_type=F32,
    )
    gap_rows = pair_gaps(
        occ_index, vir_index, eps_occ, eps_vir, row_position * rows_block, rows_block
    )
    gap_cols = pair_gaps(
        occ_index, vir_index, eps_occ, eps_vir, col_position * cols_block, cols_block
    )
    return (-gram / (gap_rows[:, None] + gap_cols[None, :])).astype(BF16)


SIDE = 4
VMEM = 50 * 2**20
ANY = pl.BlockSpec(memory_space=pl.ANY)


def dev(r, z):
    return r * SIDE + z


def plane(e):
    return [(dev(r, z), dev(r ^ e, z)) for r in range(SIDE) for z in range(SIDE)]


def deal(i):
    return [(dev(q, b), dev(b, q ^ i)) for q in range(SIDE) for b in range(SIDE)]


def send(a, edges, name):
    with jax.named_scope(name):
        return lax.ppermute(a, AXES, edges)


def after(a, *done):
    return lax.optimization_barrier((a,) + done)[0]


def chunk_sizes(depth):
    return [depth // 2] * 2


def fetch(turn, dealt, dst, sem):
    kq = dealt[0].shape[0]
    for k in range(SIDE):
        @pl.when(turn == k)
        def _(k=k):
            copies = [
                pltpu.make_async_copy(dealt[e ^ k], dst.at[pl.ds(e * kq, kq), :], sem.at[e]) for e in range(SIDE)
            ]
            for c in copies:
                c.start()
            for c in copies:
                c.wait()


def pick(turn, dealt):
    kq, width = dealt[0].shape

    def kernel(turn_ref, *rest):
        fetch(turn_ref[0], rest[:SIDE], rest[SIDE], rest[SIDE + 1])

    return pl.pallas_call(
        kernel,
        out_shape=jax.ShapeDtypeStruct((SIDE * kq, width), BF16),
        in_specs=[pl.BlockSpec(memory_space=pltpu.SMEM)] + [ANY] * SIDE,
        out_specs=pl.BlockSpec(memory_space=pltpu.VMEM),
        scratch_shapes=[pltpu.SemaphoreType.DMA((SIDE,))],
        compiler_params=pltpu.CompilerParams(vmem_limit_bytes=VMEM),
        cost_estimate=pl.CostEstimate(flops=0, bytes_accessed=4 * SIDE * kq * width, transcendentals=0),
        name="pick",
    )(turn, *dealt)


def dress(turn, dealt, amplitudes):
    kq = dealt[0].shape[0]
    depth, width = amplitudes.shape
    tile = min(512, width)

    def kernel(turn_ref, t_ref, *rest):
        dealt_refs = rest[:SIDE]
        keep, give, rows, sem = rest[SIDE:]

        @pl.when(pl.program_id(0) == 0)
        def _():
            fetch(turn_ref[0], dealt_refs, rows, sem)

        part = jnp.dot(rows[...], t_ref[...], preferred_element_type=F32)
        keep[:kq, :] = part[:kq]
        give[:kq, :] = part[kq:2 * kq].astype(give.dtype)
        keep[kq:, :] = part[2 * kq:3 * kq]
        give[kq:, :] = part[3 * kq:].astype(give.dtype)

    return pl.pallas_call(
        kernel,
        grid=(width // tile,),
        out_shape=[jax.ShapeDtypeStruct((2 * kq, width), F32), jax.ShapeDtypeStruct((2 * kq, width), BF16)],
        in_specs=[pl.BlockSpec(memory_space=pltpu.SMEM), pl.BlockSpec((depth, tile), lambda j: (0, j))] + [ANY] * SIDE,
        out_specs=[pl.BlockSpec((2 * kq, tile), lambda j: (0, j))] * 2,
        scratch_shapes=[pltpu.VMEM((SIDE * kq, depth), BF16), pltpu.SemaphoreType.DMA((SIDE,))],
        compiler_params=pltpu.CompilerParams(vmem_limit_bytes=VMEM),
        cost_estimate=pl.CostEstimate(
            flops=2 * SIDE * kq * depth * width,
            bytes_accessed=2 * depth * width + 20 * kq * width,
            transcendentals=0),
        name="dress",
    )(turn, amplitudes, *dealt)


def gram(rows, cols, gap_rows, gap_cols, partial):
    n = len(rows)
    height, width = rows[0].shape[1], cols[0].shape[1]
    depth = sum(a.shape[0] for a in rows)
    tile = min(512, height)
    strip = min(2048, width)

    def kernel(*refs):
        lhs, rhs = refs[:n], refs[n:2 * n]
        gr, gc = refs[2 * n:2 * n + 2]
        old = refs[2 * n + 2] if partial is not None else None
        out = refs[-1]
        for j in range(width // strip):
            at = pl.ds(j * strip, strip)
            total = None
            for a, b in zip(lhs, rhs):
                term = lax.dot_general(a[...], b[:, at], (((0,), (0,)), ((), ())), preferred_element_type=F32)
                total = term if total is None else total + term
            if old is not None:
                gap = gr[...] + gc[:, at]
                inverse = pl.reciprocal(gap, approx=True)
                inverse = inverse * (gap * inverse - 2.0)
                total = (total + old[:, at].astype(F32)) * inverse
            out[:, at] = total.astype(BF16)

    whole = [pl.BlockSpec(a.shape, lambda i: (0, 0)) for a in cols]
    tall = [pl.BlockSpec((a.shape[0], tile), lambda i: (0, i)) for a in rows]
    specs = tall + whole + [pl.BlockSpec((tile, 1), lambda i: (i, 0)), pl.BlockSpec((1, width), lambda i: (0, 0))]
    args = list(rows) + list(cols) + [gap_rows[:, None], gap_cols[None, :]]
    alias = {}
    if partial is not None:
        specs.append(pl.BlockSpec((tile, width), lambda i: (i, 0)))
        alias = {len(args): 0}
        args.append(partial)
    return pl.pallas_call(
        kernel,
        grid=(height // tile,),
        out_shape=jax.ShapeDtypeStruct((height, width), BF16),
        in_specs=specs,
        out_specs=pl.BlockSpec((tile, width), lambda i: (i, 0)),
        input_output_aliases=alias,
        compiler_params=pltpu.CompilerParams(vmem_limit_bytes=VMEM),
        cost_estimate=pl.CostEstimate(
            flops=2 * depth * height * width,
            bytes_accessed=(4 if partial is not None else 2) * height * width,
            transcendentals=0),
        name="gram",
    )(*args)


def four(amplitudes, cholesky, occ_index, vir_index, eps_occ, eps_vir):
    r = lax.axis_index("row")
    z = lax.axis_index("col")
    rows_block, cols_block = amplitudes.shape
    gap_rows = pair_gaps(occ_index, vir_index, eps_occ, eps_vir, r * rows_block, rows_block)
    gap_cols = pair_gaps(occ_index, vir_index, eps_occ, eps_vir, z * cols_block, cols_block)
    turn = (r ^ z).astype(jnp.int32).reshape(1)
    cat = lambda *a: jnp.concatenate(a, axis=0)
    sizes = chunk_sizes(cholesky.shape[0])
    n = len(sizes)
    own = [lax.slice_in_dim(cholesky, sum(sizes[:c]), sum(sizes[:c + 1]), axis=0) for c in range(n)]

    previous = [()] * SIDE

    def dealt(a, name, gate=()):
        got = []
        for i in range(SIDE):
            waits = previous[i] + (tuple(gate) if i == SIDE - 1 else ())
            got.append(send(after(a, *waits), deal(i), "%s_%d" % (name, i)))
        previous[:] = [(g,) for g in got]
        return got

    chol, sums, lean, other = [], [], [], []
    rows, cols = [], []

    def start_sums(c):
        keep, give = dress(after(turn, *other[-1:]), chol[c], amplitudes)
        both = keep + send(give, plane(1), "sum_core_%d" % c).astype(F32)
        mine = both[:sizes[c]] + own[c].astype(F32)
        sums.append((mine, both[sizes[c]:]))
        lean.append(cat(*sums[c]).astype(BF16))
        other.append(send(after(lean[c], *other[-1:]), plane(2), "sum_x_%d" % c))

    for c in range(n):
        chol.append(dealt(own[c], "factors_%d" % c, lean[-1:] if c >= 2 else ()))
        if c >= 1:
            start_sums(c - 1)
    start_sums(n - 1)

    early = None
    for c in range(n):
        kq = sizes[c]
        y0 = (sums[c][0] + other[c][kq:].astype(F32)).astype(BF16)
        y2 = (sums[c][1] + other[c][:kq].astype(F32)).astype(BF16)
        core = send(cat(y0, y2), plane(1), "y_core_%d" % c)
        cols.append(cat(y0, core[:kq], y2, core[kq:]))
        if c == n - 1:
            early = gram(rows, cols[:c], gap_rows, gap_cols, None)
        gate = (early,) if c == n - 1 else lean[-1:]
        rows.append(pick(turn, dealt(y0, "dressed_%d" % c, gate)))
    return gram(rows[n - 1:], cols[n - 1:], gap_rows, gap_cols, early)


def solution(mesh):
    shape = dict(mesh.shape)
    body = four if shape["row"] == SIDE and shape["col"] == SIDE else general
    return jax.shard_map(
        body,
        mesh=mesh,
        in_specs=(
            P(("grp", "row"), "col"),
            P("row", ("grp", "col")),
            P("grp"),
            P("grp"),
            P("grp"),
            P("grp"),
        ),
        out_specs=P(("grp", "row"), "col"),
        check_vma=False,
    )
```

```python
import jax
import jax.numpy as jnp
from jax import lax
from jax.experimental import pallas as pl
from jax.experimental.pallas import tpu as pltpu
from jax.sharding import PartitionSpec as P

AXES = ("row", "col")
BF16 = jnp.bfloat16
F32 = jnp.float32


def pair_gaps(occ_index, vir_index, eps_occ, eps_vir, begin_pair, pair_count):
    occ_rows = lax.dynamic_slice_in_dim(occ_index, begin_pair, pair_count, 0)
    vir_rows = lax.dynamic_slice_in_dim(vir_index, begin_pair, pair_count, 0)
    occ_table = jnp.arange(eps_occ.shape[0], dtype=jnp.int32)
    vir_table = jnp.arange(eps_vir.shape[0], dtype=jnp.int32)
    occ_energy = jnp.sum(
        jnp.where(occ_rows[:, None] == occ_table[None, :], eps_occ[None, :], 0.0), axis=1
    )
    vir_energy = jnp.sum(
        jnp.where(vir_rows[:, None] == vir_table[None, :], eps_vir[None, :], 0.0), axis=1
    )
    return vir_energy - occ_energy


def general(amplitudes, cholesky, occ_index, vir_index, eps_occ, eps_vir):
    row_position = lax.axis_index("row")
    col_position = lax.axis_index("col")
    rows_block, cols_block = amplitudes.shape
    all_pairs = lax.all_gather(cholesky, "col", axis=1, tiled=True)
    chol_rows = lax.all_to_all(all_pairs, "row", split_axis=1, concat_axis=0, tiled=True)
    dressed = lax.psum_scatter(
        jnp.dot(chol_rows, amplitudes, preferred_element_type=F32),
        "row",
        scatter_dimension=0,
        tiled=True,
    )
    ydress = (cholesky.astype(F32) + dressed).astype(BF16)
    contract = (((0,), (0,)), ((), ()))
    ydress_pairs = lax.all_gather(ydress, "col", axis=1, tiled=True)
    ydress_rows = lax.all_to_all(ydress_pairs, "row", split_axis=1, concat_axis=0, tiled=True)
    gram = lax.dot_general(
        ydress_rows,
        lax.all_gather(ydress, "row", axis=0, tiled=True),
        contract,
        preferred_element_type=F32,
    )
    gap_rows = pair_gaps(
        occ_index, vir_index, eps_occ, eps_vir, row_position * rows_block, rows_block
    )
    gap_cols = pair_gaps(
        occ_index, vir_index, eps_occ, eps_vir, col_position * cols_block, cols_block
    )
    return (-gram / (gap_rows[:, None] + gap_cols[None, :])).astype(BF16)


SIDE = 4
VMEM = 50 * 2**20
ANY = pl.BlockSpec(memory_space=pl.ANY)


def dev(r, z):
    return r * SIDE + z


def plane(e):
    return [(dev(r, z), dev(r ^ e, z)) for r in range(SIDE) for z in range(SIDE)]


def deal(i):
    return [(dev(q, b), dev(b, q ^ i)) for q in range(SIDE) for b in range(SIDE)]


def send(a, edges, name):
    with jax.named_scope(name):
        return lax.ppermute(a, AXES, edges)


def after(a, *done):
    return lax.optimization_barrier((a,) + done)[0]


def chunk_sizes(depth):
    side = 5 * depth // 16
    return [side, depth - 2 * side, side]


def fetch(turn, dealt, dst, sem):
    kq = dealt[0].shape[0]
    for k in range(SIDE):
        @pl.when(turn == k)
        def _(k=k):
            copies = [
                pltpu.make_async_copy(dealt[e ^ k], dst.at[pl.ds(e * kq, kq), :], sem.at[e]) for e in range(SIDE)
            ]
            for c in copies:
                c.start()
            for c in copies:
                c.wait()


def pick(turn, dealt):
    kq, width = dealt[0].shape

    def kernel(turn_ref, *rest):
        fetch(turn_ref[0], rest[:SIDE], rest[SIDE], rest[SIDE + 1])

    return pl.pallas_call(
        kernel,
        out_shape=jax.ShapeDtypeStruct((SIDE * kq, width), BF16),
        in_specs=[pl.BlockSpec(memory_space=pltpu.SMEM)] + [ANY] * SIDE,
        out_specs=pl.BlockSpec(memory_space=pltpu.VMEM),
        scratch_shapes=[pltpu.SemaphoreType.DMA((SIDE,))],
        compiler_params=pltpu.CompilerParams(vmem_limit_bytes=VMEM),
        cost_estimate=pl.CostEstimate(flops=0, bytes_accessed=4 * SIDE * kq * width, transcendentals=0),
        name="pick",
    )(turn, *dealt)


def dress(turn, dealt, amplitudes):
    kq = dealt[0].shape[0]
    depth, width = amplitudes.shape
    tile = min(512, width)

    def kernel(turn_ref, t_ref, *rest):
        dealt_refs = rest[:SIDE]
        keep, give, rows, sem = rest[SIDE:]

        @pl.when(pl.program_id(0) == 0)
        def _():
            fetch(turn_ref[0], dealt_refs, rows, sem)

        part = jnp.dot(rows[...], t_ref[...], preferred_element_type=F32)
        keep[:kq, :] = part[:kq]
        give[:kq, :] = part[kq:2 * kq].astype(give.dtype)
        keep[kq:, :] = part[2 * kq:3 * kq]
        give[kq:, :] = part[3 * kq:].astype(give.dtype)

    return pl.pallas_call(
        kernel,
        grid=(width // tile,),
        out_shape=[jax.ShapeDtypeStruct((2 * kq, width), F32), jax.ShapeDtypeStruct((2 * kq, width), BF16)],
        in_specs=[pl.BlockSpec(memory_space=pltpu.SMEM), pl.BlockSpec((depth, tile), lambda j: (0, j))] + [ANY] * SIDE,
        out_specs=[pl.BlockSpec((2 * kq, tile), lambda j: (0, j))] * 2,
        scratch_shapes=[pltpu.VMEM((SIDE * kq, depth), BF16), pltpu.SemaphoreType.DMA((SIDE,))],
        compiler_params=pltpu.CompilerParams(vmem_limit_bytes=VMEM),
        cost_estimate=pl.CostEstimate(
            flops=2 * SIDE * kq * depth * width,
            bytes_accessed=2 * depth * width + 20 * kq * width,
            transcendentals=0),
        name="dress",
    )(turn, amplitudes, *dealt)


def gram(rows, cols, gap_rows, gap_cols, partial):
    n = len(rows)
    height, width = rows[0].shape[1], cols[0].shape[1]
    depth = sum(a.shape[0] for a in rows)
    tile = min(512, height)
    strip = min(2048, width)

    def kernel(*refs):
        lhs, rhs = refs[:n], refs[n:2 * n]
        gr, gc = refs[2 * n:2 * n + 2]
        old = refs[2 * n + 2] if partial is not None else None
        out = refs[-1]
        for j in range(width // strip):
            at = pl.ds(j * strip, strip)
            total = None
            for a, b in zip(lhs, rhs):
                term = lax.dot_general(a[...], b[:, at], (((0,), (0,)), ((), ())), preferred_element_type=F32)
                total = term if total is None else total + term
            if old is not None:
                gap = gr[...] + gc[:, at]
                inverse = pl.reciprocal(gap, approx=True)
                inverse = inverse * (gap * inverse - 2.0)
                total = (total + old[:, at].astype(F32)) * inverse
            out[:, at] = total.astype(BF16)

    whole = [pl.BlockSpec(a.shape, lambda i: (0, 0)) for a in cols]
    tall = [pl.BlockSpec((a.shape[0], tile), lambda i: (0, i)) for a in rows]
    specs = tall + whole + [pl.BlockSpec((tile, 1), lambda i: (i, 0)), pl.BlockSpec((1, width), lambda i: (0, 0))]
    args = list(rows) + list(cols) + [gap_rows[:, None], gap_cols[None, :]]
    alias = {}
    if partial is not None:
        specs.append(pl.BlockSpec((tile, width), lambda i: (i, 0)))
        alias = {len(args): 0}
        args.append(partial)
    return pl.pallas_call(
        kernel,
        grid=(height // tile,),
        out_shape=jax.ShapeDtypeStruct((height, width), BF16),
        in_specs=specs,
        out_specs=pl.BlockSpec((tile, width), lambda i: (i, 0)),
        input_output_aliases=alias,
        compiler_params=pltpu.CompilerParams(vmem_limit_bytes=VMEM),
        cost_estimate=pl.CostEstimate(
            flops=2 * depth * height * width,
            bytes_accessed=(4 if partial is not None else 2) * height * width,
            transcendentals=0),
        name="gram",
    )(*args)


def four(amplitudes, cholesky, occ_index, vir_index, eps_occ, eps_vir):
    r = lax.axis_index("row")
    z = lax.axis_index("col")
    rows_block, cols_block = amplitudes.shape
    gap_rows = pair_gaps(occ_index, vir_index, eps_occ, eps_vir, r * rows_block, rows_block)
    gap_cols = pair_gaps(occ_index, vir_index, eps_occ, eps_vir, z * cols_block, cols_block)
    turn = (r ^ z).astype(jnp.int32).reshape(1)
    cat = lambda *a: jnp.concatenate(a, axis=0)
    sizes = chunk_sizes(cholesky.shape[0])
    n = len(sizes)
    own = [lax.slice_in_dim(cholesky, sum(sizes[:c]), sum(sizes[:c + 1]), axis=0) for c in range(n)]

    values = {}

    def stage(names):
        held = lax.optimization_barrier(tuple(values[k] for k in names))
        values.update(zip(names, held))

    def deal_out(key, source, c):
        for i in range(SIDE):
            values["%s%d_%d" % (key, c, i)] = send(values[source], deal(i), "%s_%d_%d" % (key, c, i))
        return ["%s%d_%d" % (key, c, i) for i in range(SIDE)]

    dealt = lambda key, c: [values["%s%d_%d" % (key, c, i)] for i in range(SIDE)]
    cols, rows = {}, {}
    for c in range(n):
        values["own%d" % c] = own[c]
    for t in range(2 * n):
        names = []
        if 2 <= t < n + 2:
            c = t - 2
            both = values["keep%d" % c] + send(values["give%d" % c], plane(1), "sum_core_%d" % c).astype(F32)
            values["mine%d" % c] = both[:sizes[c]] + own[c].astype(F32)
            values["second%d" % c] = both[sizes[c]:]
            lean = cat(values["mine%d" % c], values["second%d" % c]).astype(BF16)
            values["other%d" % c] = send(lean, plane(2), "sum_x_%d" % c)
            names += ["mine%d" % c, "second%d" % c, "other%d" % c]
        if t < n:
            names += deal_out("factors", "own%d" % t, t)
        if t >= n:
            c = t - n
            kq = sizes[c]
            y0 = (values["mine%d" % c] + values["other%d" % c][kq:].astype(F32)).astype(BF16)
            y2 = (values["second%d" % c] + values["other%d" % c][:kq].astype(F32)).astype(BF16)
            values["y%d" % c] = y0
            names += deal_out("dressed", "y%d" % c, c)
            core = send(cat(y0, y2), plane(1), "y_core_%d" % c)
            cols[c] = cat(y0, core[:kq], y2, core[kq:])
        if 1 <= t <= n:
            c = t - 1
            values["keep%d" % c], values["give%d" % c] = dress(values["turn"], dealt("factors", c), amplitudes)
            names += ["keep%d" % c, "give%d" % c]
        if t > n:
            c = t - n - 1
            rows[c] = pick(turn, dealt("dressed", c))
        if t == 2 * n - 1:
            at = range(n - 1)
            values["early"] = gram([rows[c] for c in at], [cols[c] for c in at], gap_rows, gap_cols, None)
            names += ["early"]
        for c in range(n):
            if c > t and c < n:
                names.append("own%d" % c)
        values.setdefault("turn", turn)
        stage(names + ["turn"])
    last = n - 1
    rows[last] = pick(turn, dealt("dressed", last))
    return gram([rows[last]], [cols[last]], gap_rows, gap_cols, values["early"])


def solution(mesh):
    shape = dict(mesh.shape)
    body = four if shape["row"] == SIDE and shape["col"] == SIDE else general
    return jax.shard_map(
        body,
        mesh=mesh,
        in_specs=(
            P(("grp", "row"), "col"),
            P("row", ("grp", "col")),
            P("grp"),
            P("grp"),
            P("grp"),
            P("grp"),
        ),
        out_specs=P(("grp", "row"), "col"),
        check_vma=False,
    )
```
